32 devices in a mesh: row: 4 (over y, x), col: 8 (over z, core).
Axes of the slice: x: 2, y: 2, z: 4, core: 2. Of those that a mesh axis runs over, the one named last changes fastest.
Arguments:
- observed: int32 [8, 768, 2048], P('col', 'row'), may hold values from 0 to 1, as said below
- user_effect: float32 [8, 768], P('col', 'row'), may hold values from -4 to 4
- item_effect: float32 [128, 128], replicated, may hold values from -4 to 4
- block_list: int32 [8, 16], replicated, may hold values from 0 to 127, as said below
Outputs:
- factored: float32 [32, 4, 128, 16, 8, 128], P(None, 'row', None, None, 'col')
- correction: bfloat16 [32, 4, 128, 16, 8, 128], P(None, 'row', None, None, 'col')
- logdet: float32 [], replicated
- pivots: float32 [4, 8, 512], P('row', 'col')
The draws below stay inside these ranges and needn't reach their ends.
Inputs may be any that keep to these rules, and one draw needn't show every extreme that they name: `block_list`: each row lists 16 distinct tiles; entry k has remainder k // (16 // 4) modulo 4; at most max(1, 16 // 8) entries of a row share a remainder modulo 8, and some remainder reaches that count in every row. `observed`: 1 marks a rating of the user for the item.
All inputs are finite; a program needn't handle non-finite values.
Results may differ from the reference program's by a relative error of at most 0.0069.
Values may be sent and summed in bfloat16 or wider, within the bound.
A program may use at most 320 MiB of HBM per device.

```python
import jax
import jax.numpy as jnp
from jax import lax

TILE = 128
ITEMS = 16384
K = 16
PANEL_BLOCKS = 2
U_DEV = 192
NB = 128
USERS = 768
N_ROW = 4
N_COL = 8


def draw_observed(key, part):
    width = K * TILE
    keys = jax.random.split(jax.random.fold_in(key, 29), 4)
    activity = jax.random.randint(keys[0], (N_COL, USERS, 1), 0, 4)
    popularity = jax.random.randint(keys[1], (N_COL, 1, width), 0, 3)
    favored = jax.random.randint(keys[2], (N_COL, USERS, 1), 0, K)
    tile_of = (jnp.arange(width, dtype=jnp.int32) // TILE)[None, None, :]
    boost = jnp.where(tile_of == favored, 3, 0).astype(jnp.int32)
    rate = jnp.left_shift(jnp.ones((), jnp.int32), (activity + popularity + boost).astype(jnp.int32))
    rolled = jax.random.randint(keys[3], (N_COL, USERS, width), 0, 2 * width)
    return (rolled < rate).astype(jnp.int32)


def draw_block_list(key, part):
    per_row = K // N_ROW
    ratio = N_COL // N_ROW
    span = ITEMS // TILE // N_COL
    first, second = jax.random.split(jax.random.fold_in(key, 17))
    offset = jax.random.randint(first, (N_COL, N_ROW, 1), 0, ratio)
    within = jnp.arange(per_row, dtype=jnp.int32)[None, None, :]
    choice_m = (within + offset) % ratio
    residue = jnp.arange(N_ROW, dtype=jnp.int32)[None, :, None] + N_ROW * choice_m
    base = jax.random.randint(second, (N_COL, N_ROW, ratio), 0, span)
    picked = jnp.take_along_axis(base, choice_m, axis=2)
    level = (picked + within // ratio) % span
    blocks = residue + N_COL * level
    return blocks.reshape(N_COL, K).astype(jnp.int32)


def block_levels(rng, dims, pieces, least, largest):
    level, own = 1.0, jax.random.fold_in(rng, 6)
    for position, blocks in pieces:
        steps = jnp.exp(jax.random.uniform(jax.random.fold_in(own, position), (blocks,), jnp.float32, least / len(pieces), largest / len(pieces)))
        level = level * jnp.repeat(steps, dims[position] // blocks).reshape([-1 if axis == position else 1 for axis in range(len(dims))])
    return level


def scatter_about(rng, shape, spread, reach, cuts=(), kind=jnp.bfloat16):
    loudness = block_levels(rng, shape, cuts, -0.22, 0.18) if cuts else 1.0
    entries = jax.random.normal(rng, shape, jnp.float32) * spread * loudness
    return jnp.minimum(jnp.maximum(entries, -reach), reach).astype(kind)


def setup_inputs(seed: int = 0) -> dict:
    key_list = jax.random.split(jax.random.key(seed), 5)
    observed = draw_observed(jax.random.fold_in(key_list[4], 71), 0)
    user_effect = scatter_about(key_list[1], (N_COL, USERS), 1.0, 4.0, ((0, 8), (1, 4)), jnp.float32)
    item_effect = scatter_about(key_list[2], (NB, TILE), 1.0, 4.0, (), jnp.float32)
    block_list = draw_block_list(jax.random.fold_in(key_list[4], 71), 0)
    return dict(observed=observed, user_effect=user_effect, item_effect=item_effect, block_list=block_list)


highest = lax.Precision.HIGHEST
user_prior = 1.0
item_prior = 1.0

def reference(observed, user_effect, item_effect, block_list):
    width = K * TILE

    def cluster(index, schur):
        blocks = lax.dynamic_index_in_dim(block_list, index, 0, keepdims=False)
        marks = lax.dynamic_index_in_dim(observed, index, 0, keepdims=False)
        effects = lax.dynamic_index_in_dim(user_effect, index, 0, keepdims=False)
        picker = (blocks[:, None] == jnp.arange(NB, dtype=jnp.int32)[None, :]).astype(jnp.float32)
        item_vals = jnp.dot(picker, item_effect, precision=highest).reshape(width)
        prob = jax.nn.sigmoid(effects[:, None] + item_vals[None, :])
        weight = jnp.where(marks > 0, prob * (1.0 - prob), 0.0)
        precision_u = user_prior + lax.optimization_barrier(jnp.sum(weight, axis=1))
        scaled = (weight / jnp.sqrt(precision_u)[:, None]).astype(jnp.bfloat16)
        col_total = lax.optimization_barrier(jnp.sum(weight, axis=0))

        def device_part(total, group):
            part = lax.dynamic_slice_in_dim(scaled, group * U_DEV, U_DEV, 0).astype(jnp.float32)
            product = jnp.dot(part.T, part, precision=highest)
            rounded = lax.optimization_barrier(product.astype(jnp.bfloat16))
            return (total + rounded.astype(jnp.float32), None)
        cross, _ = lax.scan(device_part, jnp.zeros((width, width), jnp.float32), jnp.arange(N_ROW, dtype=jnp.int32))
        block = jnp.diag(col_total) - cross
        ids = (blocks[:, None] * TILE + jnp.arange(TILE, dtype=jnp.int32)[None, :]).reshape(width).astype(jnp.int32)
        return schur.at[ids[:, None], ids[None, :]].add(block)
    schur = lax.fori_loop(0, N_COL, cluster, jnp.zeros((ITEMS, ITEMS), jnp.float32))
    schur = schur + item_prior * jnp.eye(ITEMS, dtype=jnp.float32)
    width_p = PANEL_BLOCKS * TILE
    lower = jnp.linalg.cholesky(schur[:width_p, :width_p])
    factor = lax.linalg.triangular_solve(lower, schur[:, :width_p], left_side=False, lower=True, transpose_a=True)
    logdet = 2.0 * jnp.sum(jnp.log(jnp.diagonal(lower)))
    update = jnp.dot(factor, factor.T, precision=highest)
    positions = jnp.arange(ITEMS, dtype=jnp.int32)
    below = positions >= width_p
    trailing = jnp.where(below[:, None], schur - update, 0.0)
    full = trailing.at[:, :width_p].set(factor)
    diagonal_vals = jnp.diagonal(full)
    full = full.at[positions, positions].set(0.0)
    pivots = diagonal_vals.reshape(NB // N_COL, N_COL, TILE).transpose(1, 0, 2)
    pivots = pivots.reshape(N_COL, N_ROW, ITEMS // (N_ROW * N_COL)).transpose(1, 0, 2)
    correction = jnp.where(below[:, None] & below[None, :], update, 0.0).astype(jnp.bfloat16)
    shape_out = (NB // N_ROW, N_ROW, TILE, NB // N_COL, N_COL, TILE)
    return (full.reshape(shape_out), correction.reshape(shape_out), logdet, pivots)
```

```python
import functools

import jax
import jax.numpy as jnp
from jax import lax
from jax.experimental import pallas as pl
from jax.experimental.pallas import tpu as pltpu
from jax.sharding import PartitionSpec as P

PANEL_BLOCKS = 2
EXTRA = 16
MESH = pl.DeviceIdType.MESH
HBM = pl.BlockSpec(memory_space=pl.ANY)
VMEM = pl.BlockSpec(memory_space=pltpu.VMEM)
SMEM = pl.BlockSpec(memory_space=pltpu.SMEM)

highest = lax.Precision.HIGHEST
user_prior = 1.0
item_prior = 1.0
BIG = 56 * 1024 * 1024


def dot_nt(a, b, precision=highest):
    return lax.dot_general(
        a, b, (((1,), (1,)), ((), ())), precision=precision, preferred_element_type=jnp.float32
    )


def dot_tn(a, b, precision=None):
    return lax.dot_general(
        a, b, (((0,), (0,)), ((), ())), precision=precision, preferred_element_type=jnp.float32
    )


def weight_kernel(kcount, tile, ids, blocks, observed, effect, items, out, weight):
    users = effect.shape[0]
    col = ids[1]
    user = effect[...]
    total = jnp.zeros((users, tile), jnp.float32)
    for k in range(kcount):
        span = pl.ds(k * tile, tile)
        prob = jax.nn.sigmoid(user + items[pl.ds(blocks[col, k], 1), :])
        part = jnp.where(observed[:, span] > 0, prob * (1.0 - prob), 0.0)
        weight[:, span] = part
        total = total + part
    scale = 1.0 / jnp.sqrt(user_prior + jnp.sum(total, axis=1, keepdims=True))
    line = lax.broadcasted_iota(jnp.int32, (EXTRA, tile), 0)
    for k in range(kcount):
        span = pl.ds(k * tile, tile)
        part = weight[:, span]
        out[pl.ds(0, users), span] = (part * scale).astype(jnp.bfloat16)
        sums = jnp.sum(part, axis=0, keepdims=True)
        high = sums.astype(jnp.bfloat16).astype(jnp.float32)
        mid = (sums - high).astype(jnp.bfloat16).astype(jnp.float32)
        low = sums - high - mid
        rows = jnp.where(line == 0, high, jnp.where(line == 1, mid, jnp.where(line == 2, low, 0.0)))
        out[pl.ds(users, EXTRA), span] = rows.astype(jnp.bfloat16)


def greet(peers):
    barrier = pltpu.get_barrier_semaphore()
    for peer in peers:
        pl.semaphore_signal(barrier, inc=1, device_id=peer, device_id_type=MESH)
    pl.semaphore_wait(barrier, len(peers))


def remote(src, dst, send, recv, peer):
    return pltpu.make_async_remote_copy(
        src_ref=src, dst_ref=dst, send_sem=send, recv_sem=recv, device_id=peer, device_id_type=MESH
    )


def gather_rows_kernel(rows_n, mine, out, sends, recvs, local):
    row = lax.axis_index("row")
    col = lax.axis_index("col")
    if rows_n == 4:
        x = row % 2
        y = row // 2
        px = y * 2 + (1 - x)
        py = (1 - y) * 2 + x
        pd = (1 - y) * 2 + (1 - x)
        greet([(px, col), (py, col)])
        half = mine.shape[0] // 2
        part = [pl.ds(0, half), pl.ds(half, half)]
        jobs = {}
        for n, (axis, h) in enumerate(((0, 0), (1, 1), (0, 1), (1, 0))):
            peer = (px, col) if axis == 0 else (py, col)
            jobs[(axis, h)] = remote(
                mine.at[part[h]], out.at[row, part[h]], sends.at[n], recvs.at[n], peer
            )
            jobs[(axis, h)].start()
        keep = pltpu.make_async_copy(mine, out.at[row], local)
        keep.start()
        jobs[(0, 0)].wait_recv()
        far0 = remote(out.at[px, part[0]], out.at[px, part[0]], sends.at[4], recvs.at[4], (py, col))
        far0.start()
        jobs[(1, 1)].wait_recv()
        far1 = remote(out.at[py, part[1]], out.at[py, part[1]], sends.at[5], recvs.at[5], (px, col))
        far1.start()
        jobs[(0, 1)].wait_recv()
        jobs[(1, 0)].wait_recv()
        far0.wait_recv()
        far1.wait_recv()
        for job in jobs.values():
            job.wait_send()
        far0.wait_send()
        far1.wait_send()
        keep.wait()
    else:
        peers = [(lax.rem(row + k, rows_n), col) for k in range(1, rows_n)]
        greet(peers)
        jobs = []
        for k, peer in enumerate(peers):
            jobs.append(remote(mine, out.at[row], sends.at[k], recvs.at[k], peer))
            jobs[-1].start()
        keep = pltpu.make_async_copy(mine, out.at[row], local)
        keep.start()
        for job in jobs:
            job.wait()
        keep.wait()


def product_kernel(per_row, tile, rows_n, cols_n, slots, ids, blocks, stacked, out, panel, left, count):
    users = stacked.shape[1] - EXTRA
    kcount = blocks.shape[1]
    group = per_row * tile
    row = ids[0]
    col = ids[1]
    left[...] = stacked[:, pl.ds(0, users), pl.ds(pl.multiple_of(row * group, tile), group)]
    panel[...] = jnp.zeros_like(panel)
    for c in range(cols_n):
        count[c] = 0
    eye = lax.broadcasted_iota(jnp.int32, (tile, tile), 0) == lax.broadcasted_iota(
        jnp.int32, (tile, tile), 1
    )

    @pl.loop(0, kcount)
    def _(k):
        block = blocks[col, k]
        span = pl.ds(pl.multiple_of(k * tile, tile), tile)
        cross = jnp.zeros((group, tile), jnp.float32)
        for g in range(rows_n):
            term = dot_tn(left[g], stacked[g, pl.ds(0, users), span])
            cross = cross + term.astype(jnp.bfloat16).astype(jnp.float32)
        total = jnp.zeros((1, tile), jnp.float32)
        for g in range(rows_n):
            extra = stacked[g, pl.ds(users, EXTRA), span].astype(jnp.float32)
            total = total + jnp.sum(extra, axis=0, keepdims=True)
        residue = lax.rem(block, cols_n)
        slot = count[residue]
        count[residue] = slot + 1
        place = residue * slots + jnp.minimum(slot, slots - 1)
        for j in range(per_row):
            part = -cross[j * tile : (j + 1) * tile]
            part = part + jnp.where(eye & (row * per_row + j == k), total, 0.0)
            part = part.astype(jnp.bfloat16)
            out[place, pl.ds(j * tile, tile), :] = part
            for b in range(PANEL_BLOCKS):

                @pl.when(block == b)
                def _():
                    panel[pl.ds(j * tile, tile), pl.ds(b * tile, tile)] = part


def gather_cols_kernel(cols_n, mine, out, sends, recvs, local):
    row = lax.axis_index("row")
    col = lax.axis_index("col")
    core = col % 2
    place = col // 2
    deep = cols_n // 2
    mate = (row, place * 2 + 1 - core)
    others = [lax.rem(place + k, deep) * 2 + core for k in range(1, deep)]
    greet([mate] + [(row, c) for c in others])
    jobs = []
    for k, c in enumerate(others):
        jobs.append(remote(mine, out.at[col], sends.at[k], recvs.at[k], (row, c)))
        jobs[-1].start()
    share = [remote(mine, out.at[col], sends.at[deep], recvs.at[deep], mate)]
    share[0].start()
    keep = pltpu.make_async_copy(mine, out.at[col], local)
    keep.start()
    for k in range(1, deep):
        source = lax.rem(place - k + deep, deep) * 2 + core
        jobs[k - 1].wait_recv()
        share.append(
            remote(out.at[source], out.at[source], sends.at[deep + k], recvs.at[deep + k], mate)
        )
        share[-1].start()
    for job in share:
        job.wait_recv()
    for job in jobs + share:
        job.wait_send()
    keep.wait()


def dense_kernel(per_row, tile, rows_n, ids, blocks, gathered, dense, corner, work):
    nb_r = dense.shape[0]
    cols_n = blocks.shape[0]
    row = ids[0]
    work[...] = jnp.zeros_like(work)
    shape = (tile, work.shape[2])
    first = lax.broadcasted_iota(jnp.int32, shape, 0)
    second = lax.broadcasted_iota(jnp.int32, shape, 1)
    unit = jnp.where((first + row * tile == second) & (row < PANEL_BLOCKS), item_prior, 0.0)
    work[0] = unit.astype(jnp.float32)

    @pl.loop(0, cols_n)
    def _(c):
        for j in range(per_row):
            place = blocks[c, row * per_row + j] // rows_n
            work[place] = work[place] + gathered[c, pl.ds(j * tile, tile), :].astype(jnp.float32)

    corner[...] = work[0]
    dense[...] = work[...].astype(jnp.bfloat16)


def share_rows_kernel(rows_n, dense, corner, cols, corners, sends, recvs, csends, crecvs, local):
    row = lax.axis_index("row")
    col = lax.axis_index("col")
    ratio_part = col // rows_n
    owner = lax.rem(col, rows_n)
    peers = [(lax.rem(row + k, rows_n), col) for k in range(1, rows_n)]
    greet(peers)
    for b in range(PANEL_BLOCKS):

        @pl.when(row == b)
        def _():
            for k, peer in enumerate(peers):
                remote(corner, corners.at[b], csends.at[k], crecvs.at[b], peer).start()
            pltpu.make_async_copy(corner, corners.at[b], local.at[0]).start()

    @pl.when(row == owner)
    def _():
        for k, peer in enumerate(peers):
            remote(dense.at[:, ratio_part], cols, sends.at[k], recvs.at[0], peer).start()
        pltpu.make_async_copy(dense.at[:, ratio_part], cols, local.at[1]).start()

    for b in range(PANEL_BLOCKS):

        @pl.when(row == b)
        def _():
            for k, peer in enumerate(peers):
                remote(corner, corners.at[b], csends.at[k], crecvs.at[b], peer).wait_send()
            pltpu.make_async_copy(corner, corners.at[b], local.at[0]).wait()

        @pl.when(row != b)
        def _():
            remote(corner, corners.at[b], csends.at[0], crecvs.at[b], peers[0]).wait_recv()

    @pl.when(row == owner)
    def _():
        for k, peer in enumerate(peers):
            remote(dense.at[:, ratio_part], cols, sends.at[k], recvs.at[0], peer).wait_send()
        pltpu.make_async_copy(dense.at[:, ratio_part], cols, local.at[1]).wait()

    @pl.when(row != owner)
    def _():
        remote(dense.at[:, ratio_part], cols, sends.at[0], recvs.at[0], peers[0]).wait_recv()


def eliminate(work, tile):
    first = lax.broadcasted_iota(jnp.int32, (tile, tile), 0)
    second = lax.broadcasted_iota(jnp.int32, (tile, tile), 1)
    lane = lax.broadcasted_iota(jnp.int32, (1, tile), 1)
    sub = lax.broadcasted_iota(jnp.int32, (tile, 1), 0)

    @pl.loop(0, tile)
    def _(j):
        now = work[...]
        line = work[pl.ds(j, 1), :]
        pivot = jnp.sum(jnp.where(lane == j, line, 0.0), axis=1, keepdims=True)
        column = jnp.sum(jnp.where(second == j, now, 0.0), axis=1, keepdims=True)
        factor = jnp.where(sub > j, column / pivot, 0.0)
        base = jnp.where((second == j) & (first > j), 0.0, now)
        work[...] = base - factor * jnp.where(lane == j, 1.0, line)

    done = work[...]
    eye = first == second
    pivot_col = jnp.sum(jnp.where(eye, done, 0.0), axis=1, keepdims=True)
    unit = jnp.where(eye, 1.0, jnp.where(first > second, done, 0.0))
    return unit / jnp.sqrt(pivot_col), jnp.sum(jnp.log(pivot_col), axis=0, keepdims=True)


def solve_kernel(tile, corners, dense, cols, rows_out, cols_out, exact, logdet, work, inverse):
    nb_r = dense.shape[0]
    a11 = corners[0, :, pl.ds(0, tile)]
    work[...] = a11
    w1, log1 = eliminate(work, tile)
    a21 = corners[1, :, pl.ds(0, tile)]
    l21 = dot_nt(a21, w1)
    work[...] = corners[1, :, pl.ds(tile, tile)] - dot_nt(l21, l21)
    w2, log2 = eliminate(work, tile)
    cross = jnp.dot(l21, w1, precision=highest, preferred_element_type=jnp.float32)
    w21 = -jnp.dot(w2, cross, precision=highest, preferred_element_type=jnp.float32)
    inverse[pl.ds(0, tile), pl.ds(0, tile)] = w1
    inverse[pl.ds(0, tile), pl.ds(tile, tile)] = jnp.zeros((tile, tile), jnp.float32)
    inverse[pl.ds(tile, tile), pl.ds(0, tile)] = w21
    inverse[pl.ds(tile, tile), pl.ds(tile, tile)] = w2
    logdet[...] = jnp.broadcast_to(log1 + log2, logdet.shape)
    full = inverse[...]
    high = full.astype(jnp.bfloat16)
    low = (full - high.astype(jnp.float32)).astype(jnp.bfloat16)

    def apply(block):
        return dot_nt(block, high, None) + dot_nt(block, low, None)

    @pl.loop(0, nb_r)
    def _(i):
        got = apply(dense[i])
        rows_out[i] = got.astype(jnp.bfloat16)
        exact[i] = got

    @pl.loop(0, cols.shape[0])
    def _(i):
        cols_out[i] = apply(cols[i]).astype(jnp.bfloat16)


def final_kernel(
    per_row, slots, rows_n, cols_n, ids, blocks, rows_ref, cols_ref, own_ref, tiles,
    full, corr, diag, upd, col_tab, row_cnt, row_tab
):
    i = pl.program_id(0)
    nb_r = pl.num_programs(0)
    tile = rows_ref.shape[1]
    nb_c = cols_ref.shape[0]
    kcount = blocks.shape[1]
    row = ids[0]
    col = ids[1]

    @pl.when(i == 0)
    def _():
        diag[...] = jnp.zeros_like(diag)

        @pl.loop(0, nb_r)
        def _(n):
            row_cnt[n] = 0

        @pl.loop(0, cols_n)
        def _(c):
            for s in range(slots):
                col_tab[c * slots + s] = -1

            def scan(k, seen):
                block = blocks[c, k]
                hit = lax.rem(block, cols_n) == col

                @pl.when(hit)
                def _():
                    col_tab[c * slots + jnp.minimum(seen, slots - 1)] = block // cols_n

                return seen + hit.astype(jnp.int32)

            lax.fori_loop(0, kcount, scan, jnp.int32(0))
            shift = lax.rem(col - c + cols_n, cols_n)
            for j in range(per_row):
                place = blocks[c, row * per_row + j] // rows_n
                n = row_cnt[place]
                row_cnt[place] = n + 1
                row_tab[place * cols_n + n] = c * (cols_n * per_row) + shift * per_row + j

    above = i * rows_n + row < PANEL_BLOCKS
    left = rows_ref[0]
    for jj in range(nb_c):
        upd[pl.ds(jj, tile, stride=nb_c), :] = dot_nt(left, cols_ref[jj], None)
    in_panel = col < PANEL_BLOCKS
    place = lax.rem(lax.broadcasted_iota(jnp.int32, (tile * nb_c, upd.shape[1]), 0), nb_c)

    @pl.when(above)
    def _():
        corr[0] = jnp.zeros(corr.shape[1:], corr.dtype)
        full[0] = jnp.zeros(full.shape[1:], full.dtype)

    @pl.when(jnp.logical_not(above))
    def _():
        value = upd[...]
        full[0] = -value
        corr[0] = jnp.where((place == 0) & in_panel, 0.0, value).astype(corr.dtype)

        @pl.loop(0, row_cnt[i])
        def _(n):
            code = row_tab[i * cols_n + n]
            c = code // (cols_n * per_row)
            rest = lax.rem(code, cols_n * per_row)
            shift = rest // per_row
            j = lax.rem(rest, per_row)
            for s in range(slots):
                jj = col_tab[c * slots + s]

                @pl.when(jj >= 0)
                def _():
                    part = tiles[shift, s, pl.ds(pl.multiple_of(j * tile, tile), tile), :]
                    where = pl.ds(jj, tile, stride=nb_c)
                    full[0, where, :] = full[0, where, :] + part.astype(jnp.float32)

    @pl.when(in_panel)
    def _():
        full[0, pl.ds(0, tile, stride=nb_c), :] = own_ref[0]

    far = i * rows_n + row - col

    @pl.when((far >= 0) & (lax.rem(far + cols_n * nb_c, cols_n) == 0))
    def _():
        jj = far // cols_n
        where = pl.ds(jj, tile, stride=nb_c)
        block = full[0, where, :]
        eye = lax.broadcasted_iota(jnp.int32, block.shape, 0) == lax.broadcasted_iota(
            jnp.int32, block.shape, 1
        )
        full[0, where, :] = jnp.where(eye, 0.0, block)
        prior = jnp.where(jnp.logical_or(above, in_panel & (jj == 0)), 0.0, item_prior)
        diag[pl.ds(jj, 1), :] = jnp.sum(jnp.where(eye, block, 0.0), axis=0, keepdims=True) + prior


def params(limit=BIG, **kw):
    return pltpu.CompilerParams(vmem_limit_bytes=limit, **kw)


def body(observed, user_effect, item_effect, block_list):
    rows_n = lax.axis_size("row")
    cols_n = lax.axis_size("col")
    row_idx = lax.axis_index("row")
    col_idx = lax.axis_index("col")
    nblocks, tile = item_effect.shape
    kcount = block_list.shape[1]
    per_row = kcount // rows_n
    slots = max(1, kcount // cols_n)
    width = kcount * tile
    group = per_row * tile
    nb_r = nblocks // rows_n
    nb_c = nblocks // cols_n
    users = observed.shape[1]
    width_p = PANEL_BLOCKS * tile
    ids = jnp.stack([row_idx, col_idx]).astype(jnp.int32)
    f32, bf16 = jnp.float32, jnp.bfloat16
    dma = pltpu.SemaphoreType.DMA

    mine = pl.pallas_call(
        functools.partial(weight_kernel, kcount, tile),
        out_shape=jax.ShapeDtypeStruct((users + EXTRA, width), bf16),
        in_specs=[SMEM, SMEM, VMEM, VMEM, VMEM],
        out_specs=VMEM,
        scratch_shapes=[pltpu.VMEM((users, width), f32)],
        compiler_params=params(),
        name="weights",
    )(ids, block_list, observed[0], user_effect.reshape(users, 1), item_effect)

    stacked = pl.pallas_call(
        functools.partial(gather_rows_kernel, rows_n),
        out_shape=jax.ShapeDtypeStruct((rows_n, users + EXTRA, width), bf16),
        in_specs=[HBM],
        out_specs=HBM,
        scratch_shapes=[dma((max(6, rows_n),)), dma((max(6, rows_n),)), dma],
        compiler_params=params(2**20, collective_id=0, has_side_effects=True),
        name="gather_rows",
    )(mine)

    strips, panel = pl.pallas_call(
        functools.partial(product_kernel, per_row, tile, rows_n, cols_n, slots),
        out_shape=(
            jax.ShapeDtypeStruct((cols_n * slots, group, tile), bf16),
            jax.ShapeDtypeStruct((group, width_p), bf16),
        ),
        in_specs=[SMEM, SMEM, VMEM],
        out_specs=(VMEM, VMEM),
        scratch_shapes=[pltpu.VMEM((rows_n, users, group), bf16), pltpu.SMEM((cols_n,), jnp.int32)],
        compiler_params=params(),
        name="products",
    )(ids, block_list, stacked)

    gathered = pl.pallas_call(
        functools.partial(gather_cols_kernel, cols_n),
        out_shape=jax.ShapeDtypeStruct((cols_n, group, width_p), bf16),
        in_specs=[HBM],
        out_specs=HBM,
        scratch_shapes=[dma((cols_n,)), dma((cols_n,)), dma],
        compiler_params=params(2**20, collective_id=1, has_side_effects=True),
        name="gather_cols",
    )(panel)

    strips = strips.reshape(cols_n, slots, group, tile)
    parts = [lax.dynamic_slice_in_dim(strips, col_idx, 1, 0)]
    for k in range(1, cols_n):
        part = lax.dynamic_slice_in_dim(strips, lax.rem(col_idx + k, cols_n), 1, 0)
        parts.append(lax.ppermute(part, "col", [(c, (c + k) % cols_n) for c in range(cols_n)]))
    tiles = jnp.concatenate(parts, axis=0)

    dense, corner = pl.pallas_call(
        functools.partial(dense_kernel, per_row, tile, rows_n),
        out_shape=(
            jax.ShapeDtypeStruct((nb_r, tile, width_p), bf16),
            jax.ShapeDtypeStruct((tile, width_p), f32),
        ),
        in_specs=[SMEM, SMEM, VMEM],
        out_specs=(VMEM, VMEM),
        scratch_shapes=[pltpu.VMEM((nb_r, tile, width_p), f32)],
        compiler_params=params(),
        name="dense",
    )(ids, block_list, gathered)

    ratio = cols_n // rows_n
    panel_cols, corners = pl.pallas_call(
        functools.partial(share_rows_kernel, rows_n),
        out_shape=(
            jax.ShapeDtypeStruct((nb_c, tile, width_p), bf16),
            jax.ShapeDtypeStruct((PANEL_BLOCKS, tile, width_p), f32),
        ),
        in_specs=[HBM, HBM],
        out_specs=(HBM, HBM),
        scratch_shapes=[
            dma((rows_n,)), dma((1,)), dma((rows_n,)), dma((PANEL_BLOCKS,)), dma((2,)),
        ],
        compiler_params=params(2**20, collective_id=2, has_side_effects=True),
        name="share_rows",
    )(dense.reshape(nb_c, ratio, tile, width_p), corner)

    rows_f, cols_f, exact, logs = pl.pallas_call(
        functools.partial(solve_kernel, tile),
        out_shape=(
            jax.ShapeDtypeStruct((nb_r, tile, width_p), bf16),
            jax.ShapeDtypeStruct((nb_c, tile, width_p), bf16),
            jax.ShapeDtypeStruct((nb_r, tile, width_p), f32),
            jax.ShapeDtypeStruct((8, tile), f32),
        ),
        in_specs=[VMEM, VMEM, VMEM],
        out_specs=(VMEM, VMEM, VMEM, VMEM),
        scratch_shapes=[pltpu.VMEM((tile, tile), f32), pltpu.VMEM((width_p, width_p), f32)],
        compiler_params=params(),
        name="solve",
    )(corners, dense, panel_cols)
    logdet = logs[0, 0]

    rows_all = tile * nb_c
    full, corr, diag = pl.pallas_call(
        functools.partial(final_kernel, per_row, slots, rows_n, cols_n),
        grid_spec=pltpu.PrefetchScalarGridSpec(
            num_scalar_prefetch=2,
            grid=(nb_r,),
            in_specs=[
                pl.BlockSpec((1, tile, width_p), lambda i, ids, bl: (i, 0, 0)),
                pl.BlockSpec((nb_c, tile, width_p), lambda i, ids, bl: (0, 0, 0)),
                pl.BlockSpec(
                    (1, tile, tile), lambda i, ids, bl: (i, 0, jnp.minimum(ids[1], PANEL_BLOCKS - 1))
                ),
                pl.BlockSpec((cols_n, slots, group, tile), lambda i, ids, bl: (0, 0, 0, 0)),
            ],
            out_specs=[
                pl.BlockSpec((1, rows_all, tile), lambda i, ids, bl: (i, 0, 0)),
                pl.BlockSpec((1, rows_all, tile), lambda i, ids, bl: (i, 0, 0)),
                pl.BlockSpec((nb_c, tile), lambda i, ids, bl: (0, 0)),
            ],
            scratch_shapes=[
                pltpu.VMEM((rows_all, tile), f32),
                pltpu.SMEM((cols_n * slots,), jnp.int32),
                pltpu.SMEM((nb_r,), jnp.int32),
                pltpu.SMEM((nb_r * cols_n,), jnp.int32),
            ],
        ),
        out_shape=(
            jax.ShapeDtypeStruct((nb_r, rows_all, tile), f32),
            jax.ShapeDtypeStruct((nb_r, rows_all, tile), bf16),
            jax.ShapeDtypeStruct((nb_c, tile), f32),
        ),
        compiler_params=params(),
        name="final",
    )(ids, block_list, rows_f, cols_f, exact, tiles)

    pivot_part = lax.psum_scatter(diag.reshape(nb_c * tile), "row", scatter_dimension=0, tiled=True)
    pivots = pivot_part.reshape(1, 1, pivot_part.shape[0])
    out = (nb_r, 1, tile, nb_c, 1, tile)
    return (full.reshape(out), corr.reshape(out), logdet, pivots)


def solution(mesh):
    in_specs = (P("col", "row", None), P("col", "row"), P(), P())
    out_specs = (
        P(None, "row", None, None, "col", None),
        P(None, "row", None, None, "col", None),
        P(),
        P("row", "col", None),
    )
    return jax.shard_map(body, mesh=mesh, in_specs=in_specs, out_specs=out_specs, check_vma=False)
```

```python
import functools

import jax
import jax.numpy as jnp
from jax import lax
from jax.experimental import pallas as pl
from jax.experimental.pallas import tpu as pltpu
from jax.sharding import PartitionSpec as P

PANEL_BLOCKS = 2
EXTRA = 16
MESH = pl.DeviceIdType.MESH
HBM = pl.BlockSpec(memory_space=pl.ANY)
VMEM = pl.BlockSpec(memory_space=pltpu.VMEM)
SMEM = pl.BlockSpec(memory_space=pltpu.SMEM)

highest = lax.Precision.HIGHEST
user_prior = 1.0
item_prior = 1.0
BIG = 56 * 1024 * 1024


def dot_nt(a, b, precision=highest):
    return lax.dot_general(
        a, b, (((1,), (1,)), ((), ())), precision=precision, preferred_element_type=jnp.float32
    )


def dot_tn(a, b, precision=None):
    return lax.dot_general(
        a, b, (((0,), (0,)), ((), ())), precision=precision, preferred_element_type=jnp.float32
    )


def weight_kernel(kcount, tile, ids, blocks, observed, effect, items, out, weight):
    users = effect.shape[0]
    col = ids[1]
    user = effect[...]
    total = jnp.zeros((users, tile), jnp.float32)
    for k in range(kcount):
        span = pl.ds(k * tile, tile)
        prob = jax.nn.sigmoid(user + items[pl.ds(blocks[col, k], 1), :])
        part = jnp.where(observed[:, span] > 0, prob * (1.0 - prob), 0.0)
        weight[:, span] = part
        total = total + part
    scale = 1.0 / jnp.sqrt(user_prior + jnp.sum(total, axis=1, keepdims=True))
    line = lax.broadcasted_iota(jnp.int32, (EXTRA, tile), 0)
    for k in range(kcount):
        span = pl.ds(k * tile, tile)
        part = weight[:, span]
        out[pl.ds(0, users), span] = (part * scale).astype(jnp.bfloat16)
        sums = jnp.sum(part, axis=0, keepdims=True)
        high = sums.astype(jnp.bfloat16).astype(jnp.float32)
        mid = (sums - high).astype(jnp.bfloat16).astype(jnp.float32)
        low = sums - high - mid
        rows = jnp.where(line == 0, high, jnp.where(line == 1, mid, jnp.where(line == 2, low, 0.0)))
        out[pl.ds(users, EXTRA), span] = rows.astype(jnp.bfloat16)


def greet(peers):
    barrier = pltpu.get_barrier_semaphore()
    for peer in peers:
        pl.semaphore_signal(barrier, inc=1, device_id=peer, device_id_type=MESH)
    pl.semaphore_wait(barrier, len(peers))


def remote(src, dst, send, recv, peer):
    return pltpu.make_async_remote_copy(
        src_ref=src, dst_ref=dst, send_sem=send, recv_sem=recv, device_id=peer, device_id_type=MESH
    )


def gather_rows_kernel(rows_n, mine, out, sends, recvs, local):
    row = lax.axis_index("row")
    col = lax.axis_index("col")
    if rows_n == 4:
        x = row % 2
        y = row // 2
        px = y * 2 + (1 - x)
        py = (1 - y) * 2 + x
        pd = (1 - y) * 2 + (1 - x)
        greet([(px, col), (py, col)])
        half = mine.shape[0] // 2
        part = [pl.ds(0, half), pl.ds(half, half)]
        jobs = {}
        for n, (axis, h) in enumerate(((0, 0), (1, 1), (0, 1), (1, 0))):
            peer = (px, col) if axis == 0 else (py, col)
            jobs[(axis, h)] = remote(
                mine.at[part[h]], out.at[row, part[h]], sends.at[n], recvs.at[n], peer
            )
            jobs[(axis, h)].start()
        keep = pltpu.make_async_copy(mine, out.at[row], local)
        keep.start()
        jobs[(0, 0)].wait_recv()
        far0 = remote(out.at[px, part[0]], out.at[px, part[0]], sends.at[4], recvs.at[4], (py, col))
        far0.start()
        jobs[(1, 1)].wait_recv()
        far1 = remote(out.at[py, part[1]], out.at[py, part[1]], sends.at[5], recvs.at[5], (px, col))
        far1.start()
        jobs[(0, 1)].wait_recv()
        jobs[(1, 0)].wait_recv()
        far0.wait_recv()
        far1.wait_recv()
        for job in jobs.values():
            job.wait_send()
        far0.wait_send()
        far1.wait_send()
        keep.wait()
    else:
        peers = [(lax.rem(row + k, rows_n), col) for k in range(1, rows_n)]
        greet(peers)
        jobs = []
        for k, peer in enumerate(peers):
            jobs.append(remote(mine, out.at[row], sends.at[k], recvs.at[k], peer))
            jobs[-1].start()
        keep = pltpu.make_async_copy(mine, out.at[row], local)
        keep.start()
        for job in jobs:
            job.wait()
        keep.wait()


def product_kernel(per_row, tile, rows_n, cols_n, slots, ids, blocks, stacked, out, panel, left, count):
    users = stacked.shape[1] - EXTRA
    kcount = blocks.shape[1]
    group = per_row * tile
    row = ids[0]
    col = ids[1]
    left[...] = stacked[:, pl.ds(0, users), pl.ds(pl.multiple_of(row * group, tile), group)]
    panel[...] = jnp.zeros_like(panel)
    for c in range(cols_n):
        count[c] = 0
    eye = lax.broadcasted_iota(jnp.int32, (tile, tile), 0) == lax.broadcasted_iota(
        jnp.int32, (tile, tile), 1
    )

    @pl.loop(0, kcount)
    def _(k):
        block = blocks[col, k]
        span = pl.ds(pl.multiple_of(k * tile, tile), tile)
        cross = jnp.zeros((group, tile), jnp.float32)
        for g in range(rows_n):
            term = dot_tn(left[g], stacked[g, pl.ds(0, users), span])
            cross = cross + term.astype(jnp.bfloat16).astype(jnp.float32)
        total = jnp.zeros((1, tile), jnp.float32)
        for g in range(rows_n):
            extra = stacked[g, pl.ds(users, EXTRA), span].astype(jnp.float32)
            total = total + jnp.sum(extra, axis=0, keepdims=True)
        residue = lax.rem(block, cols_n)
        slot = count[residue]
        count[residue] = slot + 1
        place = residue * slots + jnp.minimum(slot, slots - 1)
        for j in range(per_row):
            part = -cross[j * tile : (j + 1) * tile]
            part = part + jnp.where(eye & (row * per_row + j == k), total, 0.0)
            part = part.astype(jnp.bfloat16)
            out[place, pl.ds(j * tile, tile), :] = part
            for b in range(PANEL_BLOCKS):

                @pl.when(block == b)
                def _():
                    panel[pl.ds(j * tile, tile), pl.ds(b * tile, tile)] = part


def gather_cols_kernel(cols_n, mine, out, sends, recvs, local):
    row = lax.axis_index("row")
    col = lax.axis_index("col")
    core = col % 2
    place = col // 2
    deep = cols_n // 2
    mate = (row, place * 2 + 1 - core)
    others = [lax.rem(place + k, deep) * 2 + core for k in range(1, deep)]
    greet([mate] + [(row, c) for c in others])
    jobs = []
    for k, c in enumerate(others):
        jobs.append(remote(mine, out.at[col], sends.at[k], recvs.at[k], (row, c)))
        jobs[-1].start()
    share = [remote(mine, out.at[col], sends.at[deep], recvs.at[deep], mate)]
    share[0].start()
    keep = pltpu.make_async_copy(mine, out.at[col], local)
    keep.start()
    for k in range(1, deep):
        source = lax.rem(place - k + deep, deep) * 2 + core
        jobs[k - 1].wait_recv()
        share.append(
            remote(out.at[source], out.at[source], sends.at[deep + k], recvs.at[deep + k], mate)
        )
        share[-1].start()
    for job in share:
        job.wait_recv()
    for job in jobs + share:
        job.wait_send()
    keep.wait()


def dense_kernel(per_row, tile, rows_n, ids, blocks, gathered, dense, corner, work):
    nb_r = dense.shape[0]
    cols_n = blocks.shape[0]
    row = ids[0]
    work[...] = jnp.zeros_like(work)
    shape = (tile, work.shape[2])
    first = lax.broadcasted_iota(jnp.int32, shape, 0)
    second = lax.broadcasted_iota(jnp.int32, shape, 1)
    unit = jnp.where((first + row * tile == second) & (row < PANEL_BLOCKS), item_prior, 0.0)
    work[0] = unit.astype(jnp.float32)

    @pl.loop(0, cols_n)
    def _(c):
        for j in range(per_row):
            place = blocks[c, row * per_row + j] // rows_n
            work[place] = work[place] + gathered[c, pl.ds(j * tile, tile), :].astype(jnp.float32)

    corner[...] = work[0]
    dense[...] = work[...].astype(jnp.bfloat16)


def share_rows_kernel(
    rows_n, cols_n, near_n, dense, corner, strips, cols, corners, near,
    sends, recvs, csends, crecvs, local, nsends, nrecvs
):
    row = lax.axis_index("row")
    col = lax.axis_index("col")
    ratio_part = col // rows_n
    owner = lax.rem(col, rows_n)
    peers = [(lax.rem(row + k, rows_n), col) for k in range(1, rows_n)]
    greet(peers + [(row, lax.rem(col - k + cols_n, cols_n)) for k in range(1, near_n + 1)])
    tiles = []
    for k in range(1, near_n + 1):
        target = lax.rem(col + k, cols_n)
        tiles.append(
            remote(
                strips.at[target], near.at[k - 1], nsends.at[k - 1], nrecvs.at[k - 1], (row, target)
            )
        )
    for b in range(PANEL_BLOCKS):

        @pl.when(row == b)
        def _():
            for k, peer in enumerate(peers):
                remote(corner, corners.at[b], csends.at[k], crecvs.at[b], peer).start()
            pltpu.make_async_copy(corner, corners.at[b], local.at[0]).start()

    @pl.when(row == owner)
    def _():
        for k, peer in enumerate(peers):
            remote(dense.at[:, ratio_part], cols, sends.at[k], recvs.at[0], peer).start()
        pltpu.make_async_copy(dense.at[:, ratio_part], cols, local.at[1]).start()

    for job in tiles:
        job.start()
    for b in range(PANEL_BLOCKS):

        @pl.when(row == b)
        def _():
            for k, peer in enumerate(peers):
                remote(corner, corners.at[b], csends.at[k], crecvs.at[b], peer).wait_send()
            pltpu.make_async_copy(corner, corners.at[b], local.at[0]).wait()

        @pl.when(row != b)
        def _():
            remote(corner, corners.at[b], csends.at[0], crecvs.at[b], peers[0]).wait_recv()

    @pl.when(row == owner)
    def _():
        for k, peer in enumerate(peers):
            remote(dense.at[:, ratio_part], cols, sends.at[k], recvs.at[0], peer).wait_send()
        pltpu.make_async_copy(dense.at[:, ratio_part], cols, local.at[1]).wait()

    @pl.when(row != owner)
    def _():
        remote(dense.at[:, ratio_part], cols, sends.at[0], recvs.at[0], peers[0]).wait_recv()

    for job in tiles:
        job.wait()


def eliminate(work, tile):
    first = lax.broadcasted_iota(jnp.int32, (tile, tile), 0)
    second = lax.broadcasted_iota(jnp.int32, (tile, tile), 1)
    lane = lax.broadcasted_iota(jnp.int32, (1, tile), 1)
    sub = lax.broadcasted_iota(jnp.int32, (tile, 1), 0)

    many = 4

    @pl.loop(0, tile // many)
    def _(step):
        start = step * many
        now = work[...]
        rows = [work[pl.ds(start + a, 1), :] for a in range(many)]
        cols = [
            jnp.sum(jnp.where(second == start + a, now, 0.0), axis=1, keepdims=True)
            for a in range(many)
        ]
        small = [
            [
                jnp.sum(jnp.where(lane == start + b, rows[a], 0.0), axis=1, keepdims=True)
                for b in range(many)
            ]
            for a in range(many)
        ]
        after = sub >= start + many
        inside = (second >= start) & (second < start + many) & (first >= start + many)
        base = jnp.where(inside, 0.0, now)
        for a in range(many):
            inv = 1.0 / small[a][a]
            fixed = jnp.where(lane == start + a, 1.0, rows[a])
            scale = jnp.where(after, cols[a] * inv, 0.0)
            below = (lane > start + a) & (lane < start + many)
            base = base - scale * jnp.where(below, 0.0, fixed)
            for b in range(a + 1, many):
                ratio = small[b][a] * inv
                rows[b] = jnp.where(lane == start + a, 0.0, rows[b]) - ratio * fixed
                cols[b] = cols[b] - scale * small[a][b]
                for c in range(a + 1, many):
                    small[b][c] = small[b][c] - ratio * small[a][c]
        work[...] = base
        for a in range(1, many):
            work[pl.ds(start + a, 1), :] = rows[a]

    done = work[...]
    eye = first == second
    pivot_col = jnp.sum(jnp.where(eye, done, 0.0), axis=1, keepdims=True)
    unit = jnp.where(eye, 1.0, jnp.where(first > second, done, 0.0))
    return unit / jnp.sqrt(pivot_col), jnp.sum(jnp.log(pivot_col), axis=0, keepdims=True)


def solve_kernel(tile, corners, dense, cols, rows_out, cols_out, exact, logdet, work, inverse):
    nb_r = dense.shape[0]
    a11 = corners[0, :, pl.ds(0, tile)]
    work[...] = a11
    w1, log1 = eliminate(work, tile)
    a21 = corners[1, :, pl.ds(0, tile)]
    l21 = dot_nt(a21, w1)
    work[...] = corners[1, :, pl.ds(tile, tile)] - dot_nt(l21, l21)
    w2, log2 = eliminate(work, tile)
    cross = jnp.dot(l21, w1, precision=highest, preferred_element_type=jnp.float32)
    w21 = -jnp.dot(w2, cross, precision=highest, preferred_element_type=jnp.float32)
    inverse[pl.ds(0, tile), pl.ds(0, tile)] = w1
    inverse[pl.ds(0, tile), pl.ds(tile, tile)] = jnp.zeros((tile, tile), jnp.float32)
    inverse[pl.ds(tile, tile), pl.ds(0, tile)] = w21
    inverse[pl.ds(tile, tile), pl.ds(tile, tile)] = w2
    logdet[...] = jnp.broadcast_to(log1 + log2, logdet.shape)
    full = inverse[...]
    high = full.astype(jnp.bfloat16)
    low = (full - high.astype(jnp.float32)).astype(jnp.bfloat16)

    def apply(block):
        return dot_nt(block, high, None) + dot_nt(block, low, None)

    @pl.loop(0, nb_r)
    def _(i):
        got = apply(dense[i])
        rows_out[i] = got.astype(jnp.bfloat16)
        exact[i] = got

    for i in range(cols.shape[0]):
        got = dot_nt(high, cols[i], None) + dot_nt(low, cols[i], None)
        cols_out[:, pl.ds(i * tile, tile)] = got.astype(jnp.bfloat16)


def final_kernel(
    per_row, slots, rows_n, cols_n, batch, ids, blocks, rows_ref, cols_ref, own_ref, tiles,
    full, corr, diag, upd, col_tab, row_cnt, row_tab
):
    first = pl.program_id(0) * batch
    nb_r = pl.num_programs(0) * batch
    tile = rows_ref.shape[1]
    nb_c = cols_ref.shape[1] // tile
    kcount = blocks.shape[1]
    row = ids[0]
    col = ids[1]

    @pl.when(first == 0)
    def _():
        diag[...] = jnp.zeros_like(diag)

        @pl.loop(0, nb_r)
        def _(n):
            row_cnt[n] = 0

        @pl.loop(0, cols_n)
        def _(c):
            for s in range(slots):
                col_tab[c * slots + s] = -1

            def scan(k, seen):
                block = blocks[c, k]
                hit = lax.rem(block, cols_n) == col

                @pl.when(hit)
                def _():
                    col_tab[c * slots + jnp.minimum(seen, slots - 1)] = block // cols_n

                return seen + hit.astype(jnp.int32)

            lax.fori_loop(0, kcount, scan, jnp.int32(0))
            shift = lax.rem(col - c + cols_n, cols_n)
            for j in range(per_row):
                place = blocks[c, row * per_row + j] // rows_n
                n = row_cnt[place]
                row_cnt[place] = n + 1
                row_tab[place * cols_n + n] = c * (cols_n * per_row) + shift * per_row + j

    left = rows_ref[...].reshape(batch * tile, rows_ref.shape[2])
    pair = 2
    for jj in range(0, nb_c, pair):
        got = jnp.dot(
            left, cols_ref[:, pl.ds(jj * tile, pair * tile)], preferred_element_type=jnp.float32
        )
        for u in range(batch):
            for v in range(pair):
                part = got[u * tile : (u + 1) * tile, v * tile : (v + 1) * tile]
                upd[u, pl.ds(jj + v, tile, stride=nb_c), :] = part

    for u in range(batch):
        i = first + u
        above = i * rows_n + row < PANEL_BLOCKS
        in_panel = col < PANEL_BLOCKS
        place = lax.rem(lax.broadcasted_iota(jnp.int32, (tile * nb_c, upd.shape[2]), 0), nb_c)

        @pl.when(above)
        def _():
            corr[u] = jnp.zeros(corr.shape[1:], corr.dtype)
            full[u] = jnp.zeros(full.shape[1:], full.dtype)

        @pl.when(jnp.logical_not(above))
        def _():
            value = upd[u]
            full[u] = -value
            corr[u] = jnp.where((place == 0) & in_panel, 0.0, value).astype(corr.dtype)

            @pl.loop(0, row_cnt[i])
            def _(n):
                code = row_tab[i * cols_n + n]
                c = code // (cols_n * per_row)
                rest = lax.rem(code, cols_n * per_row)
                shift = rest // per_row
                j = lax.rem(rest, per_row)
                for s in range(slots):
                    jj = col_tab[c * slots + s]

                    @pl.when(jj >= 0)
                    def _():
                        part = tiles[shift, s, pl.ds(pl.multiple_of(j * tile, tile), tile), :]
                        where = pl.ds(jj, tile, stride=nb_c)
                        full[u, where, :] = full[u, where, :] + part.astype(jnp.float32)

        @pl.when(in_panel)
        def _():
            full[u, pl.ds(0, tile, stride=nb_c), :] = own_ref[u]

        far = i * rows_n + row - col

        @pl.when((far >= 0) & (lax.rem(far + cols_n * nb_c, cols_n) == 0))
        def _():
            jj = far // cols_n
            where = pl.ds(jj, tile, stride=nb_c)
            block = full[u, where, :]
            eye = lax.broadcasted_iota(jnp.int32, block.shape, 0) == lax.broadcasted_iota(
                jnp.int32, block.shape, 1
            )
            full[u, where, :] = jnp.where(eye, 0.0, block)
            prior = jnp.where(jnp.logical_or(above, in_panel & (jj == 0)), 0.0, item_prior)
            diag[pl.ds(jj, 1), :] = jnp.sum(jnp.where(eye, block, 0.0), axis=0, keepdims=True) + prior


def params(limit=BIG, **kw):
    return pltpu.CompilerParams(vmem_limit_bytes=limit, **kw)


def body(observed, user_effect, item_effect, block_list):
    rows_n = lax.axis_size("row")
    cols_n = lax.axis_size("col")
    row_idx = lax.axis_index("row")
    col_idx = lax.axis_index("col")
    nblocks, tile = item_effect.shape
    kcount = block_list.shape[1]
    per_row = kcount // rows_n
    slots = max(1, kcount // cols_n)
    width = kcount * tile
    group = per_row * tile
    nb_r = nblocks // rows_n
    nb_c = nblocks // cols_n
    users = observed.shape[1]
    width_p = PANEL_BLOCKS * tile
    ids = jnp.stack([row_idx, col_idx]).astype(jnp.int32)
    f32, bf16 = jnp.float32, jnp.bfloat16
    dma = pltpu.SemaphoreType.DMA

    mine = pl.pallas_call(
        functools.partial(weight_kernel, kcount, tile),
        out_shape=jax.ShapeDtypeStruct((users + EXTRA, width), bf16),
        in_specs=[SMEM, SMEM, VMEM, VMEM, VMEM],
        out_specs=VMEM,
        scratch_shapes=[pltpu.VMEM((users, width), f32)],
        compiler_params=params(),
        name="weights",
    )(ids, block_list, observed[0], user_effect.reshape(users, 1), item_effect)

    stacked = pl.pallas_call(
        functools.partial(gather_rows_kernel, rows_n),
        out_shape=jax.ShapeDtypeStruct((rows_n, users + EXTRA, width), bf16),
        in_specs=[HBM],
        out_specs=HBM,
        scratch_shapes=[dma((max(6, rows_n),)), dma((max(6, rows_n),)), dma],
        compiler_params=params(2**20, collective_id=0, has_side_effects=True),
        name="gather_rows",
    )(mine)

    strips, panel = pl.pallas_call(
        functools.partial(product_kernel, per_row, tile, rows_n, cols_n, slots),
        out_shape=(
            jax.ShapeDtypeStruct((cols_n * slots, group, tile), bf16),
            jax.ShapeDtypeStruct((group, width_p), bf16),
        ),
        in_specs=[SMEM, SMEM, VMEM],
        out_specs=(VMEM, VMEM),
        scratch_shapes=[pltpu.VMEM((rows_n, users, group), bf16), pltpu.SMEM((cols_n,), jnp.int32)],
        compiler_params=params(),
        name="products",
    )(ids, block_list, stacked)

    gathered = pl.pallas_call(
        functools.partial(gather_cols_kernel, cols_n),
        out_shape=jax.ShapeDtypeStruct((cols_n, group, width_p), bf16),
        in_specs=[HBM],
        out_specs=HBM,
        scratch_shapes=[dma((cols_n,)), dma((cols_n,)), dma],
        compiler_params=params(2**20, collective_id=1, has_side_effects=True),
        name="gather_cols",
    )(panel)

    strips, gathered = lax.optimization_barrier((strips, gathered))
    strips = strips.reshape(cols_n, slots, group, tile)
    near_n = min(3, cols_n - 1)
    parts = [lax.dynamic_slice_in_dim(strips, col_idx, 1, 0)]
    for k in range(near_n + 1, cols_n):
        part = lax.dynamic_slice_in_dim(strips, lax.rem(col_idx + k, cols_n), 1, 0)
        parts.append(lax.ppermute(part, "col", [(c, (c + k) % cols_n) for c in range(cols_n)]))

    dense, corner = pl.pallas_call(
        functools.partial(dense_kernel, per_row, tile, rows_n),
        out_shape=(
            jax.ShapeDtypeStruct((nb_r, tile, width_p), bf16),
            jax.ShapeDtypeStruct((tile, width_p), f32),
        ),
        in_specs=[SMEM, SMEM, VMEM],
        out_specs=(VMEM, VMEM),
        scratch_shapes=[pltpu.VMEM((nb_r, tile, width_p), f32)],
        compiler_params=params(),
        name="dense",
    )(ids, block_list, gathered)

    ratio = cols_n // rows_n
    panel_cols, corners, near = pl.pallas_call(
        functools.partial(share_rows_kernel, rows_n, cols_n, near_n),
        out_shape=(
            jax.ShapeDtypeStruct((nb_c, tile, width_p), bf16),
            jax.ShapeDtypeStruct((PANEL_BLOCKS, tile, width_p), f32),
            jax.ShapeDtypeStruct((near_n, slots, group, tile), bf16),
        ),
        in_specs=[HBM, HBM, HBM],
        out_specs=(HBM, HBM, HBM),
        scratch_shapes=[
            dma((rows_n,)), dma((1,)), dma((rows_n,)), dma((PANEL_BLOCKS,)), dma((2,)),
            dma((near_n,)), dma((near_n,)),
        ],
        compiler_params=params(2**20, collective_id=2, has_side_effects=True),
        name="share_rows",
    )(dense.reshape(nb_c, ratio, tile, width_p), corner, strips)
    tiles = jnp.concatenate([parts[0], near] + parts[1:], axis=0)

    rows_f, cols_f, exact, logs = pl.pallas_call(
        functools.partial(solve_kernel, tile),
        out_shape=(
            jax.ShapeDtypeStruct((nb_r, tile, width_p), bf16),
            jax.ShapeDtypeStruct((width_p, nb_c * tile), bf16),
            jax.ShapeDtypeStruct((nb_r, tile, width_p), f32),
            jax.ShapeDtypeStruct((8, tile), f32),
        ),
        in_specs=[VMEM, VMEM, VMEM],
        out_specs=(VMEM, VMEM, VMEM, VMEM),
        scratch_shapes=[pltpu.VMEM((tile, tile), f32), pltpu.VMEM((width_p, width_p), f32)],
        compiler_params=params(),
        name="solve",
    )(corners, dense, panel_cols)
    logdet = logs[0, 0]

    rows_all = tile * nb_c
    batch = 2
    full, corr, diag = pl.pallas_call(
        functools.partial(final_kernel, per_row, slots, rows_n, cols_n, batch),
        grid_spec=pltpu.PrefetchScalarGridSpec(
            num_scalar_prefetch=2,
            grid=(nb_r // batch,),
            in_specs=[
                pl.BlockSpec((batch, tile, width_p), lambda i, ids, bl: (i, 0, 0)),
                pl.BlockSpec((width_p, nb_c * tile), lambda i, ids, bl: (0, 0)),
                pl.BlockSpec(
                    (batch, tile, tile), lambda i, ids, bl: (i, 0, jnp.minimum(ids[1], PANEL_BLOCKS - 1))
                ),
                pl.BlockSpec((cols_n, slots, group, tile), lambda i, ids, bl: (0, 0, 0, 0)),
            ],
            out_specs=[
                pl.BlockSpec((batch, rows_all, tile), lambda i, ids, bl: (i, 0, 0)),
                pl.BlockSpec((batch, rows_all, tile), lambda i, ids, bl: (i, 0, 0)),
                pl.BlockSpec((nb_c, tile), lambda i, ids, bl: (0, 0)),
            ],
            scratch_shapes=[
                pltpu.VMEM((batch, rows_all, tile), f32),
                pltpu.SMEM((cols_n * slots,), jnp.int32),
                pltpu.SMEM((nb_r,), jnp.int32),
                pltpu.SMEM((nb_r * cols_n,), jnp.int32),
            ],
        ),
        out_shape=(
            jax.ShapeDtypeStruct((nb_r, rows_all, tile), f32),
            jax.ShapeDtypeStruct((nb_r, rows_all, tile), bf16),
            jax.ShapeDtypeStruct((nb_c, tile), f32),
        ),
        compiler_params=params(),
        name="final",
    )(ids, block_list, rows_f, cols_f, exact, tiles)

    pivot_part = lax.psum_scatter(diag.reshape(nb_c * tile), "row", scatter_dimension=0, tiled=True)
    pivots = pivot_part.reshape(1, 1, pivot_part.shape[0])
    out = (nb_r, 1, tile, nb_c, 1, tile)
    return (full.reshape(out), corr.reshape(out), logdet, pivots)


def solution(mesh):
    in_specs = (P("col", "row", None), P("col", "row"), P(), P())
    out_specs = (
        P(None, "row", None, None, "col", None),
        P(None, "row", None, None, "col", None),
        P(),
        P("row", "col", None),
    )
    return jax.shard_map(body, mesh=mesh, in_specs=in_specs, out_specs=out_specs, check_vma=False)
```
